32 devices in a mesh: tm: 4 (over y, x), rows: 8 (over z, core).
Axes of the slice: x: 2, y: 2, z: 4, core: 2. Of those that a mesh axis runs over, the one named last changes fastest.
Arguments:
- frames: bfloat16 [8, 128, 128, 512], P('tm', 'rows'), may hold values from -6 to 6
- space_weight: bfloat16 [3, 3, 512, 512], replicated, may hold values from -0.09375 to 0.09375
- time_weight: bfloat16 [3, 512, 2, 256], replicated, may hold values from -0.15625 to 0.15625
- out_weight: bfloat16 [3, 3, 256, 256], replicated, may hold values from -0.125 to 0.125
Outputs:
- decoded: bfloat16 [16, 128, 128, 256], P('tm', 'rows')
The draws below stay inside these ranges and needn't reach their ends.
All inputs are finite; a program needn't handle non-finite values.
Results may differ from the reference program's by a relative error of at most 0.0095.
Values may be sent and summed in bfloat16 or wider, within the bound.
No kernel may reach another device: no remote copies, remote signals or barrier semaphores. Data moves between devices by JAX's collectives and lax.ppermute only.
A program may use at most 128 MiB of HBM per device.

```python
import jax
import jax.numpy as jnp
from jax import lax

CH_IN = 512
CH_OUT = 256
WIDTH = 128
FRAMES = 8
HEIGHT = 128


def levels(own_key, extent, split, smallest, high):
    def one(axis_at, shards_of):
        heights = jax.random.uniform(jax.random.fold_in(jax.random.fold_in(own_key, 6), axis_at), (shards_of,), jnp.float32, smallest / len(split), high / len(split))
        return jnp.repeat(jnp.exp(heights), extent[axis_at] // shards_of).reshape((-1,) + (1,) * (len(extent) - axis_at - 1))

    loudness = one(*split[0])
    for cut in split[1:]:
        loudness = loudness * one(*cut)
    return loudness


def centred(own_key, extent, deviation, bound, pieces=(), kind=jnp.bfloat16):
    level = levels(own_key, extent, pieces, -0.22, 0.18) if pieces else 1.0
    array = jax.random.normal(own_key, extent, jnp.float32) * deviation * level
    return jnp.minimum(jnp.maximum(array, -bound), bound).astype(kind)


def setup_inputs(seed: int = 0) -> dict:
    key_of = jax.random.split(jax.random.key(seed), 5)
    return {
        "frames": centred(key_of[0], (FRAMES, HEIGHT, WIDTH, CH_IN), 1.0, 6.0, ((0, 4), (1, 8))),
        "space_weight": centred(key_of[1], (3, 3, CH_IN, CH_IN), (9 * CH_IN) ** -0.5, 0.09375),
        "time_weight": centred(key_of[2], (3, CH_IN, 2, CH_OUT), (3 * CH_IN) ** -0.5, 0.15625),
        "out_weight": centred(key_of[3], (3, 3, CH_OUT, CH_OUT), (9 * CH_OUT) ** -0.5, 0.125),
    }


def conv_three(field, kernel):
    return lax.conv_general_dilated(field, kernel, (1, 1), ((1, 1), (1, 1)), dimension_numbers=("NHWC", "HWIO", "NHWC"), preferred_element_type=jnp.float32)


def reference(frames, space_weight, time_weight, out_weight):
    act_in = jax.nn.silu(frames.astype(jnp.float32)).astype(jnp.bfloat16)
    hidden = (frames.astype(jnp.float32) + conv_three(act_in, space_weight)).astype(jnp.bfloat16)
    padded = jnp.pad(hidden, ((2, 0), (0, 0), (0, 0), (0, 0)))
    total = jnp.einsum("frwc,ced->ferwd", padded[0:FRAMES].astype(jnp.float32), time_weight[0].astype(jnp.float32))
    total = total + jnp.einsum("frwc,ced->ferwd", padded[1:FRAMES + 1].astype(jnp.float32), time_weight[1].astype(jnp.float32))
    total = total + jnp.einsum("frwc,ced->ferwd", padded[2:FRAMES + 2].astype(jnp.float32), time_weight[2].astype(jnp.float32))
    upsampled = total.reshape((2 * FRAMES, HEIGHT, WIDTH, CH_OUT)).astype(jnp.bfloat16)
    act_up = jax.nn.silu(upsampled.astype(jnp.float32)).astype(jnp.bfloat16)
    return (upsampled.astype(jnp.float32) + conv_three(act_up, out_weight)).astype(jnp.bfloat16)
```

```python
import functools

import jax
import jax.numpy as jnp
from jax import lax
from jax.experimental import pallas as pl
from jax.experimental.pallas import tpu as pltpu
from jax.sharding import PartitionSpec as P

MIB = 1024 * 1024


def silu(v):
    half = 0.5 * v
    return half + half * jnp.tanh(half)


def activate_row(x_ref, act_ref, row, frame):
    width, channels = x_ref.shape[2:]
    step = 256
    column = lax.broadcasted_iota(jnp.int32, (width, step), 0)
    for start in range(0, channels, step):
        v = x_ref[row, frame, :, start : start + step].astype(jnp.float32)
        a = silu(v)
        before = jnp.where(column == 0, 0.0, pltpu.roll(a, 1, 0))
        after = jnp.where(column == width - 1, 0.0, pltpu.roll(a, width - 1, 0))
        act_ref[row, frame, :, start : start + step] = before.astype(jnp.bfloat16)
        act_ref[row, frame, :, channels + start : channels + start + step] = a.astype(jnp.bfloat16)
        act_ref[row, frame, :, 2 * channels + start : 2 * channels + start + step] = after.astype(
            jnp.bfloat16
        )


def conv_group(x_ref, act_ref, w_ref, out_ref, source, target, group, ready):
    _, frames, width, channels = x_ref.shape
    size = group * frames * width
    total = x_ref[pl.ds(source + 1, group)].reshape(size, channels).astype(jnp.float32)
    for tap in range(3):
        ready(tap)
        lhs = act_ref[pl.ds(source + tap, group)].reshape(size, 3 * channels)
        total += jnp.dot(lhs, w_ref[tap], preferred_element_type=jnp.float32)
    out_ref[pl.ds(target, group)] = total.astype(jnp.bfloat16).reshape(group, frames, width, channels)


def residual_kernel(plan, *refs):
    sources = refs[: plan["sources"]]
    w_hbm = refs[plan["sources"]]
    outs = refs[plan["first_out"] : plan["first_out"] + plan["outs"]]
    x_ref, act_ref, w_ref, out_ref, edge_ref, in_sem, w_sem, out_sem, edge_sem = refs[
        plan["first_out"] + plan["outs"] :
    ]
    frames = x_ref.shape[1]

    for source, frame_major, start, count, target in plan["loads"]:
        for row in range(count):
            if frame_major:
                for frame in range(frames):
                    pltpu.make_async_copy(
                        sources[source].at[frame, start + row], x_ref.at[target + row, frame], in_sem.at[target + row]
                    ).start()
            else:
                pltpu.make_async_copy(
                    sources[source].at[start + row], x_ref.at[target + row], in_sem.at[target + row]
                ).start()
    if plan["held"]:
        weights, w_ref = [], w_hbm
    else:
        weights = [pltpu.make_async_copy(w_hbm.at[tap], w_ref.at[tap], w_sem.at[tap]) for tap in range(3)]
    edges = [
        (
            pltpu.make_async_copy(sources[0].at[:, pl.ds(row, 1)], edge_ref.at[number], edge_sem.at[number]),
            pltpu.make_async_copy(
                edge_ref.at[number], outs[plan["outs"] - len(plan["edges"]) + number], edge_sem.at[number]
            ),
        )
        for number, row in enumerate(plan["edges"])
    ]
    for copy in weights:
        copy.start()
    for fetch, _ in edges:
        fetch.start()

    def activate(row):
        pltpu.make_async_copy(x_ref.at[row], x_ref.at[row], in_sem.at[row]).wait()

        def body(frame, carry):
            activate_row(x_ref, act_ref, row, frame)
            return carry

        lax.fori_loop(0, frames, body, 0)

    def store(out, frame_major, start, count, row):
        if frame_major:
            return [
                pltpu.make_async_copy(
                    out_ref.at[pl.ds(row, count), frame], outs[out].at[frame, pl.ds(start, count)], out_sem.at[0]
                )
                for frame in range(frames)
            ]
        return [
            pltpu.make_async_copy(out_ref.at[pl.ds(row, count)], outs[out].at[pl.ds(start, count)], out_sem.at[0])
        ]

    for copy in weights:
        copy.wait()
    for fetch, hand_on in edges:
        fetch.wait()
        hand_on.start()
    target = 0
    for source, count, active, out, frame_major, start in plan["runs"]:
        group = min(count, 2)
        for row in range(active, 2):
            activate(source + row)

        def body(step, carry, source=source, target=target, group=group, out=out, frame_major=frame_major, start=start):
            for row in range(group):
                activate(source + step * group + 2 + row)
            conv_group(
                x_ref, act_ref, w_ref, out_ref, source + step * group, target + step * group, group, lambda tap: None
            )
            for copy in store(out, frame_major, start + step * group, group, target + step * group):
                copy.start()
            return carry

        lax.fori_loop(0, count // group, body, 0)
        target += count

    pltpu.make_async_copy(out_ref, out_ref, out_sem.at[0]).wait()
    for _, hand_on in edges:
        hand_on.wait()


def residual(name, sources, weight, loads, runs, out_shapes, dims, into=None, after=(), edges=(), held=True):
    frames, width, channels = dims
    rows_in = max(target + count for *_, count, target in loads)
    rows_out = sum(run[1] for run in runs)
    args = list(sources) + [weight] + list(after) + ([] if into is None else [into])
    out_shapes = list(out_shapes) + [(frames, 1, width, channels)] * len(edges)
    plan = dict(
        sources=len(sources), first_out=len(args), outs=len(out_shapes), loads=loads, runs=runs, edges=edges, held=held
    )
    flops = 2 * rows_out * frames * width * 9 * channels * channels
    return pl.pallas_call(
        functools.partial(residual_kernel, plan),
        out_shape=[jax.ShapeDtypeStruct(shape, jnp.bfloat16) for shape in out_shapes],
        in_specs=[
            pl.BlockSpec(memory_space=pltpu.VMEM if held and arg is weight else pl.ANY) for arg in args
        ],
        out_specs=[pl.BlockSpec(memory_space=pl.ANY)] * len(out_shapes),
        scratch_shapes=[
            pltpu.VMEM((rows_in, frames, width, channels), jnp.bfloat16),
            pltpu.VMEM((rows_in, frames, width, 3 * channels), jnp.bfloat16),
            pltpu.VMEM((16, 128) if held else (3, 3 * channels, channels), jnp.bfloat16),
            pltpu.VMEM((rows_out, frames, width, channels), jnp.bfloat16),
            pltpu.VMEM((2, frames, 1, width, channels) if edges else (16, 128), jnp.bfloat16),
            pltpu.SemaphoreType.DMA((rows_in,)),
            pltpu.SemaphoreType.DMA((3,)),
            pltpu.SemaphoreType.DMA((1,)),
            pltpu.SemaphoreType.DMA((2,)),
        ],
        input_output_aliases={} if into is None else {len(args) - 1: 0},
        compiler_params=pltpu.CompilerParams(
            vmem_limit_bytes=2 * frames * width * channels * (4 * rows_in + rows_out) + 12 * MIB
        ),
        cost_estimate=pl.CostEstimate(
            flops=flops,
            bytes_accessed=2 * (rows_in + rows_out) * frames * width * channels + 18 * channels * channels,
            transcendentals=rows_in * frames * width * channels,
        ),
        name=name,
    )(*args)


def upsample_kernel(own_ref, prev_ref, w_ref, _, out_ref):
    rows, _, width, channels = own_ref.shape
    depth = out_ref.shape[3]
    size = rows * width
    window = [
        prev_ref[:, 0].reshape(size, channels),
        prev_ref[:, 1].reshape(size, channels),
        own_ref[:, 0].reshape(size, channels),
        own_ref[:, 1].reshape(size, channels),
    ]
    for frame in range(2):
        total = jnp.dot(window[frame], w_ref[0], preferred_element_type=jnp.float32)
        for tap in (1, 2):
            total += jnp.dot(window[frame + tap], w_ref[tap], preferred_element_type=jnp.float32)
        total = total.astype(jnp.bfloat16)
        for half in range(2):
            out_ref[:, 2 * frame + half] = total[:, half * depth : (half + 1) * depth].reshape(
                rows, width, depth
            )


def upsample(name, own, prev, weight, depth, after):
    rows, frames, width, channels = own.shape
    block = min(rows, 2)
    return pl.pallas_call(
        upsample_kernel,
        grid=(rows // block,),
        out_shape=jax.ShapeDtypeStruct((rows, 2 * frames, width, depth), jnp.bfloat16),
        in_specs=[
            pl.BlockSpec((block, frames, width, channels), lambda i: (i, 0, 0, 0)),
            pl.BlockSpec((block, frames, width, channels), lambda i: (i, 0, 0, 0)),
            pl.BlockSpec(weight.shape, lambda i: (0, 0, 0)),
            pl.BlockSpec(memory_space=pl.ANY),
        ],
        out_specs=pl.BlockSpec((block, 2 * frames, width, depth), lambda i: (i, 0, 0, 0)),
        compiler_params=pltpu.CompilerParams(vmem_limit_bytes=12 * MIB),
        cost_estimate=pl.CostEstimate(
            flops=2 * rows * frames * width * 3 * channels * 2 * depth,
            bytes_accessed=2 * rows * frames * width * (2 * channels + 2 * depth) + 2 * weight.size,
            transcendentals=0,
        ),
        name=name,
    )(own, prev, weight, after)


def to_next(value, axis):
    count = lax.axis_size(axis)
    return lax.ppermute(value, axis, [(i, i + 1) for i in range(count - 1)])


def to_previous(value, axis):
    count = lax.axis_size(axis)
    return lax.ppermute(value, axis, [(i + 1, i) for i in range(count - 1)])


def on_device(frames, space_weight, time_weight, out_weight):
    count, rows, width, channels = frames.shape
    depth = time_weight.shape[3]
    space = space_weight.reshape(3, 3 * channels, channels)
    time = time_weight.reshape(3, channels, 2 * depth)
    out_w = out_weight.reshape(3, 3 * depth, depth)
    wide = (count, width, channels)
    fine = (2 * count, width, depth)
    last = rows - 1

    def chunk(n):
        return (n, count, width, channels)

    (ha,) = residual(
        "hidden_1_2", [frames], space, [(0, True, 0, 4, 0)], [(0, 2, 0, 0, False, 0)], [chunk(2)], wide, held=False
    )
    pa = to_next(ha, "tm")
    hb, first_row, last_row = residual(
        "hidden_3_6", [frames], space, [(0, True, 2, 6, 0)], [(0, 4, 0, 0, False, 0)], [chunk(4)], wide,
        after=[ha], edges=(0, last),
    )
    pb = to_next(hb, "tm")
    above = to_next(last_row, "rows")
    below = to_previous(first_row, "rows")
    (hc,) = residual(
        "hidden_7_10", [frames], space, [(0, True, 6, 6, 0)], [(0, 4, 0, 0, False, 0)], [chunk(4)], wide, after=[hb]
    )
    pc = to_next(hc, "tm")
    hd, he, hf = residual(
        "hidden_rest",
        [frames, above, below],
        space,
        [(1, True, 0, 1, 0), (0, True, 0, 2, 1), (0, True, 10, 6, 3), (2, True, 0, 1, 9)],
        [(0, 1, 0, 0, False, 1), (3, 2, 0, 1, False, 0), (5, 2, 2, 2, False, 0), (7, 1, 2, 0, False, 0)],
        [chunk(2), chunk(2), chunk(2)],
        wide,
        after=[hc],
    )
    pd = to_next(hd, "tm")
    pe = to_next(he, "tm")
    pf = to_next(hf, "tm")

    out_shape = [(2 * count, rows, width, depth)]
    ua = upsample("up_a", ha, pa, time, depth, hd)
    ub = upsample("up_b", hb, pb, time, depth, ua)
    (out,) = residual(
        "out_2_5", [ua, ub], out_w, [(0, False, 0, 2, 0), (1, False, 0, 4, 2)], [(0, 4, 0, 0, True, 2)], out_shape, fine
    )
    uc = upsample("up_c", hc, pc, time, depth, out)
    (out,) = residual(
        "out_6_9", [ub, uc], out_w, [(0, False, 2, 2, 0), (1, False, 0, 4, 2)], [(0, 4, 0, 0, True, 6)], out_shape, fine,
        into=out,
    )
    ud = upsample("up_d", hd, pd, time, depth, uc)
    up_above = to_next(ud[:1], "rows")
    up_below = to_previous(ud[1:], "rows")
    ue = upsample("up_e", he, pe, time, depth, ud)
    (out,) = residual(
        "out_0_1_10_11",
        [ua, uc, ud, ue, up_above],
        out_w,
        [(1, False, 2, 2, 0), (3, False, 0, 2, 2), (4, False, 0, 1, 4), (2, False, 1, 1, 5), (0, False, 0, 2, 6)],
        [(0, 2, 0, 0, True, 10), (4, 2, 0, 0, True, 0)],
        out_shape,
        fine,
        into=out,
    )
    uf = upsample("up_f", hf, pf, time, depth, ue)
    (out,) = residual(
        "out_12_15",
        [ue, uf, ud, up_below],
        out_w,
        [(0, False, 0, 2, 0), (1, False, 0, 2, 2), (2, False, 0, 1, 4), (3, False, 0, 1, 5)],
        [(0, 4, 0, 0, True, 12)],
        out_shape,
        fine,
        into=out,
    )
    return out


def solution(mesh):
    return jax.shard_map(
        on_device,
        mesh=mesh,
        in_specs=(P("tm", "rows", None, None), P(), P(), P()),
        out_specs=P("tm", "rows", None, None),
        check_vma=False,
    )
```

```python
import functools

import jax
import jax.numpy as jnp
from jax import lax
from jax.experimental import pallas as pl
from jax.experimental.pallas import tpu as pltpu
from jax.sharding import PartitionSpec as P

MIB = 1024 * 1024


def silu(v):
    half = 0.5 * v
    return half + half * jnp.tanh(half)


def activate(x_ref, act_ref, row, frame):
    width, channels = x_ref.shape[2:]
    step = 256
    column = lax.broadcasted_iota(jnp.int32, (width, step), 0)
    for start in range(0, channels, step):
        v = x_ref[row, frame, :, start : start + step].astype(jnp.float32)
        a = silu(v)
        before = jnp.where(column == 0, 0.0, pltpu.roll(a, 1, 0))
        after = jnp.where(column == width - 1, 0.0, pltpu.roll(a, width - 1, 0))
        for tap, value in enumerate((before, a, after)):
            act_ref[row, frame, :, tap * channels + start : tap * channels + start + step] = value.astype(
                jnp.bfloat16
            )


def convolve(x_ref, act_ref, w_ref, out_ref, source, target, group, between):
    _, frames, width, channels = x_ref.shape
    size = group * frames * width
    total = x_ref[pl.ds(source + 1, group)].reshape(size, channels).astype(jnp.float32)
    for tap in range(3):
        between(tap)
        lhs = act_ref[pl.ds(source + tap, group)].reshape(size, 3 * channels)
        total += jnp.dot(lhs, w_ref[tap], preferred_element_type=jnp.float32)
    out_ref[pl.ds(target, group)] = total.astype(jnp.bfloat16).reshape(group, frames, width, channels)


def lift(own_ref, before_ref, time_ref, x_ref, source, target, count):
    _, frames, width, channels = own_ref.shape
    depth = x_ref.shape[3]
    size = count * width
    window = [
        ref[pl.ds(source, count), frame].reshape(size, channels)
        for ref in (before_ref, own_ref)
        for frame in range(frames)
    ]
    for frame in range(frames):
        total = None
        for tap in range(3):
            part = jnp.dot(window[frame + tap], time_ref[tap], preferred_element_type=jnp.float32)
            total = part if total is None else total + part
        total = total.astype(jnp.bfloat16)
        for half in range(2):
            x_ref[pl.ds(target, count), 2 * frame + half] = total[:, half * depth : (half + 1) * depth].reshape(
                count, width, depth
            )


def stage_kernel(plan, *refs):
    refs = list(refs)
    sources = [refs.pop(0) for _ in range(plan["sources"])]
    w_ref = refs.pop(0)
    time_ref = refs.pop(0) if plan["lifts"] else None
    for _ in range(plan["unread"]):
        refs.pop(0)
    outs = [refs.pop(0) for _ in range(plan["outs"])]
    x_ref, act_ref = [refs.pop(0) for _ in range(2)]
    frames = x_ref.shape[1]

    fetched = plan["fetched"]
    if fetched:
        in_sem = refs.pop(0)
        for source, start, count, target in plan["loads"]:
            for row in range(count):
                for frame in range(frames):
                    pltpu.make_async_copy(
                        sources[source].at[frame, start + row], x_ref.at[target + row, frame], in_sem.at[target + row]
                    ).start()
    weights = []
    if plan["fetch"]:
        w_hbm = w_ref
        w_ref, w_sem = [refs.pop(0) for _ in range(2)]
        weights = [pltpu.make_async_copy(w_hbm.at[tap], w_ref.at[tap], w_sem.at[tap]) for tap in range(3)]
    edges = []
    if plan["edges"]:
        edge_sem = refs.pop(0)
        edges = [
            pltpu.make_async_copy(
                sources[0].at[:, pl.ds(row, 1)], outs[plan["outs"] - len(plan["edges"]) + number], edge_sem.at[number]
            )
            for number, row in enumerate(plan["edges"])
        ]
    for copy in weights + edges:
        copy.start()
    if plan["staged"]:
        stage_ref, out_sem = [refs.pop(0) for _ in range(2)]

    for own, before, start, count, target in plan["lifts"]:
        step = min(count, 2)

        def body(number, carry, own=own, before=before, start=start, target=target, step=step):
            lift(
                sources[own], sources[before], time_ref, x_ref, start + number * step, target + number * step, step
            )
            return carry

        lax.fori_loop(0, count // step, body, 0)
    if not fetched:
        for source, start, count, target in plan["loads"]:
            x_ref[pl.ds(target, count)] = sources[source][pl.ds(start, count)]
    for out, row, count in plan["keeps"]:
        outs[out][...] = x_ref[pl.ds(row, count)]

    def prepare(row, frame):
        if fetched and frame == 0:
            pltpu.make_async_copy(x_ref.at[row], x_ref.at[row], in_sem.at[row]).wait()
        activate(x_ref, act_ref, row, frame)

    target = 0
    for number, (source, count, active, out, start) in enumerate(plan["runs"]):
        group = min(count, 2)
        steps = count // group

        def first(row, carry, source=source):
            for frame in range(frames):
                prepare(source + row, frame)
            return carry

        lax.fori_loop(active, group + 2, first, 0)

        def body(step, carry, last, source=source, target=target, group=group, out=out, start=start):
            def between(tap):
                if weights and number == 0 and last:
                    weights[tap].wait()
                if last:
                    return
                for at, (row, frame) in enumerate((r, f) for r in range(group) for f in range(frames)):
                    if at * 3 // (group * frames) == tap:
                        prepare(source + (step + 1) * group + 2 + row, frame)

            row = target + step * group if plan["staged"] else start + step * group
            to_ref = stage_ref if plan["staged"] else outs[out]
            convolve(x_ref, act_ref, w_ref, to_ref, source + step * group, row, group, between)
            if plan["staged"]:
                for frame in range(frames):
                    pltpu.make_async_copy(
                        stage_ref.at[pl.ds(row, group), frame],
                        outs[out].at[frame, pl.ds(start + step * group, group)],
                        out_sem.at[0],
                    ).start()
            return carry

        if steps > 1:
            lax.fori_loop(0, steps - 1, functools.partial(body, last=False), 0)
        body(steps - 1, 0, last=True)
        target += count

    if plan["staged"]:
        pltpu.make_async_copy(stage_ref, stage_ref, out_sem.at[0]).wait()
    for copy in edges:
        copy.wait()


def stage(
    name,
    sources,
    weight,
    loads,
    runs,
    out_shapes,
    dims,
    fetched=False,
    staged=False,
    lifts=(),
    time=None,
    keeps=(),
    into=None,
    after=(),
    edges=(),
    fetch=False,
):
    frames, width, channels = dims
    rows_in = max(target + count for *_, count, target in list(loads) + list(lifts))
    rows_out = sum(run[1] for run in runs)
    args = list(sources) + [weight]
    spaces = [pl.ANY if fetched else pltpu.VMEM] * len(sources) + [pltpu.HBM if fetch else pltpu.VMEM]
    if lifts:
        args.append(time)
        spaces.append(pltpu.VMEM)
    unread = list(after) + ([] if into is None else [into])
    args += unread
    spaces += [pl.ANY] * len(unread)
    out_spaces = [pltpu.HBM if staged else pltpu.VMEM] + [pltpu.VMEM] * (len(out_shapes) - 1 + len(edges))
    out_shapes = list(out_shapes) + [(frames, 1, width, channels)] * len(edges)
    plan = dict(
        sources=len(sources),
        unread=len(unread),
        outs=len(out_shapes),
        loads=loads,
        fetched=fetched,
        staged=staged,
        lifts=lifts,
        keeps=keeps,
        runs=runs,
        edges=edges,
        fetch=fetch,
    )
    scratch = [
        pltpu.VMEM((rows_in, frames, width, channels), jnp.bfloat16),
        pltpu.VMEM((rows_in, frames, width, 3 * channels), jnp.bfloat16),
    ]
    held = 2 * frames * width * channels * 4 * rows_in
    flops = 2 * rows_out * frames * width * 9 * channels * channels
    if lifts:
        flops += 2 * sum(entry[3] for entry in lifts) * frames * width * 3 * time.shape[1] * channels
    if fetched:
        scratch.append(pltpu.SemaphoreType.DMA((rows_in,)))
    if fetch:
        scratch += [pltpu.VMEM(weight.shape, jnp.bfloat16), pltpu.SemaphoreType.DMA((3,))]
        held += 2 * weight.size
    if edges:
        scratch.append(pltpu.SemaphoreType.DMA((len(edges),)))
    if staged:
        scratch += [pltpu.VMEM((rows_out, frames, width, channels), jnp.bfloat16), pltpu.SemaphoreType.DMA((1,))]
        held += 2 * frames * width * channels * rows_out
    return pl.pallas_call(
        functools.partial(stage_kernel, plan),
        out_shape=[jax.ShapeDtypeStruct(shape, jnp.bfloat16) for shape in out_shapes],
        in_specs=[pl.BlockSpec(memory_space=space) for space in spaces],
        out_specs=[pl.BlockSpec(memory_space=space) for space in out_spaces],
        scratch_shapes=scratch,
        input_output_aliases={} if into is None else {len(args) - 1: 0},
        compiler_params=pltpu.CompilerParams(vmem_limit_bytes=held + 12 * MIB),
        cost_estimate=pl.CostEstimate(flops=flops, bytes_accessed=1024, transcendentals=0),
        name=name,
    )(*args)


def to_next(value, axis):
    count = lax.axis_size(axis)
    return lax.ppermute(value, axis, [(i, i + 1) for i in range(count - 1)])


def to_previous(value, axis):
    count = lax.axis_size(axis)
    return lax.ppermute(value, axis, [(i + 1, i) for i in range(count - 1)])


def on_device(frames, space_weight, time_weight, out_weight):
    count, rows, width, channels = frames.shape
    depth = time_weight.shape[3]
    space = space_weight.reshape(3, 3 * channels, channels)
    time = time_weight.reshape(3, channels, 2 * depth)
    out_w = out_weight.reshape(3, 3 * depth, depth)
    wide = (count, width, channels)
    fine = (2 * count, width, depth)
    last = rows - 1

    def chunk(n):
        return (n, count, width, channels)

    def lifted(n):
        return (n, 2 * count, width, depth)

    here = pltpu.with_memory_space_constraint(frames, pltpu.HBM)
    space_here = pltpu.with_memory_space_constraint(space, pltpu.HBM)
    (ha,) = stage(
        "hidden_1_2", [here], space_here, [(0, 0, 4, 0)], [(0, 2, 0, 0, 0)], [chunk(2)], wide, fetched=True, fetch=True
    )
    pa = to_next(ha, "tm")
    (hb,) = stage(
        "hidden_3_6",
        [here],
        space,
        [(0, 2, 6, 0)],
        [(0, 4, 0, 0, 0)],
        [chunk(4)],
        wide,
        fetched=True,
        after=[ha],
    )
    pb = to_next(hb, "tm")
    hc, first_row, last_row = stage(
        "hidden_7_10",
        [here],
        space,
        [(0, 6, 6, 0)],
        [(0, 4, 0, 0, 0)],
        [chunk(4)],
        wide,
        fetched=True,
        after=[hb],
        edges=(0, last),
    )
    pc = to_next(hc, "tm")
    above = to_next(last_row, "rows")
    below = to_previous(first_row, "rows")
    hd, he, hf = stage(
        "hidden_rest",
        [here, above, below],
        space,
        [(1, 0, 1, 0), (0, 0, 2, 1), (0, 10, 6, 3), (2, 0, 1, 9)],
        [(0, 1, 0, 0, 1), (3, 2, 0, 1, 0), (5, 2, 2, 2, 0), (7, 1, 2, 0, 0)],
        [chunk(2), chunk(2), chunk(2)],
        wide,
        fetched=True,
        after=[hc, pa],
    )
    pd = to_next(hd, "tm")
    pe = to_next(he, "tm")
    pf = to_next(hf, "tm")

    whole = (2 * count, rows, width, depth)
    out, ua, ub = stage(
        "out_2_5",
        [ha, pa, hb, pb],
        out_w,
        [],
        [(0, 4, 0, 0, 2)],
        [whole, lifted(2), lifted(2)],
        fine,
        staged=True,
        lifts=[(0, 1, 0, 2, 0), (2, 3, 0, 4, 2)],
        time=time,
        keeps=[(1, 0, 2), (2, 4, 2)],
        after=[hd],
    )
    out, uc = stage(
        "out_6_9",
        [hc, pc, ub],
        out_w,
        [(2, 0, 2, 0)],
        [(0, 4, 0, 0, 6)],
        [whole, lifted(2)],
        fine,
        staged=True,
        lifts=[(0, 1, 0, 4, 2)],
        time=time,
        keeps=[(1, 4, 2)],
        into=out,
    )
    ud = upsample("up_edges", hd, pd, time, depth, uc)
    up_above = to_next(ud[:1], "rows")
    up_below = to_previous(ud[1:], "rows")
    out, ue = stage(
        "out_0_1_10_11",
        [he, pe, uc, ua, ud, up_above],
        out_w,
        [(2, 0, 2, 0), (5, 0, 1, 4), (4, 1, 1, 5), (3, 0, 2, 6)],
        [(0, 2, 0, 0, 10), (4, 2, 0, 0, 0)],
        [whole, lifted(2)],
        fine,
        staged=True,
        lifts=[(0, 1, 0, 2, 2)],
        time=time,
        keeps=[(1, 2, 2)],
        into=out,
    )
    (out,) = stage(
        "out_12_15",
        [hf, pf, ue, ud, up_below],
        out_w,
        [(2, 0, 2, 0), (3, 0, 1, 4), (4, 0, 1, 5)],
        [(0, 4, 0, 0, 12)],
        [whole],
        fine,
        staged=True,
        lifts=[(0, 1, 0, 2, 2)],
        time=time,
        into=out,
    )
    return out


def upsample_kernel(own_ref, prev_ref, w_ref, _, out_ref):
    rows, _, width, channels = own_ref.shape
    depth = out_ref.shape[3]
    size = rows * width
    window = [
        prev_ref[:, 0].reshape(size, channels),
        prev_ref[:, 1].reshape(size, channels),
        own_ref[:, 0].reshape(size, channels),
        own_ref[:, 1].reshape(size, channels),
    ]
    for frame in range(2):
        total = jnp.dot(window[frame], w_ref[0], preferred_element_type=jnp.float32)
        for tap in (1, 2):
            total += jnp.dot(window[frame + tap], w_ref[tap], preferred_element_type=jnp.float32)
        total = total.astype(jnp.bfloat16)
        for half in range(2):
            out_ref[:, 2 * frame + half] = total[:, half * depth : (half + 1) * depth].reshape(
                rows, width, depth
            )


def upsample(name, own, prev, weight, depth, after):
    rows, frames, width, channels = own.shape
    return pl.pallas_call(
        upsample_kernel,
        out_shape=jax.ShapeDtypeStruct((rows, 2 * frames, width, depth), jnp.bfloat16),
        in_specs=[pl.BlockSpec(memory_space=pltpu.VMEM)] * 3 + [pl.BlockSpec(memory_space=pltpu.HBM)],
        out_specs=pl.BlockSpec(memory_space=pltpu.VMEM),
        compiler_params=pltpu.CompilerParams(vmem_limit_bytes=12 * MIB),
        cost_estimate=pl.CostEstimate(
            flops=2 * rows * frames * width * 3 * channels * 2 * depth,
            bytes_accessed=2 * rows * frames * width * (2 * channels + 2 * depth) + 2 * weight.size,
            transcendentals=0,
        ),
        name=name,
    )(own, prev, weight, after)


def solution(mesh):
    return jax.shard_map(
        on_device,
        mesh=mesh,
        in_specs=(P("tm", "rows", None, None), P(), P(), P()),
        out_specs=P("tm", "rows", None, None),
        check_vma=False,
    )
```

```python
import functools

import jax
import jax.numpy as jnp
from jax import lax
from jax.experimental import pallas as pl
from jax.experimental.pallas import tpu as pltpu
from jax.sharding import PartitionSpec as P

MIB = 1024 * 1024


def silu(v):
    half = 0.5 * v
    return half + half * jnp.tanh(half)


def activate(x_ref, act_ref, row, frame):
    width, channels = x_ref.shape[2:]
    step = 256
    column = lax.broadcasted_iota(jnp.int32, (width, step), 0)
    for start in range(0, channels, step):
        v = x_ref[row, frame, :, start : start + step].astype(jnp.float32)
        a = silu(v)
        before = jnp.where(column == 0, 0.0, pltpu.roll(a, 1, 0))
        after = jnp.where(column == width - 1, 0.0, pltpu.roll(a, width - 1, 0))
        for tap, value in enumerate((before, a, after)):
            act_ref[row, frame, :, tap * channels + start : tap * channels + start + step] = value.astype(
                jnp.bfloat16
            )


def convolve(x_ref, act_ref, w_ref, out_ref, source, target, group, between, parts=None):
    _, frames, width, channels = x_ref.shape
    size = group * frames * width
    total = None
    for tap in range(3):
        between(tap)
        if parts is None:
            lhs = act_ref[pl.ds(source + tap, group)].reshape(size, 3 * channels)
            part = jnp.dot(lhs, w_ref[tap], preferred_element_type=jnp.float32)
            total = part if total is None else total + part
            continue
        for column in range(3):
            parts[3 * tap + column].wait()
            if tap == 0 and column == 2:
                for copy in parts[6:]:
                    copy.start()
            span = slice(column * channels, (column + 1) * channels)
            lhs = act_ref[pl.ds(source + tap, group), :, :, span].reshape(size, channels)
            part = jnp.dot(lhs, w_ref[tap, span], preferred_element_type=jnp.float32)
            total = part if total is None else total + part
    total += x_ref[pl.ds(source + 1, group)].reshape(size, channels).astype(jnp.float32)
    out_ref[pl.ds(target, group)] = total.astype(jnp.bfloat16).reshape(group, frames, width, channels)


def lift(own_ref, before_ref, time_ref, x_ref, source, target, count):
    _, frames, width, channels = own_ref.shape
    depth = x_ref.shape[3]
    size = count * width
    window = [
        ref[pl.ds(source, count), frame].reshape(size, channels)
        for ref in (before_ref, own_ref)
        for frame in range(frames)
    ]
    for frame in range(frames):
        total = None
        for tap in range(3):
            part = jnp.dot(window[frame + tap], time_ref[tap], preferred_element_type=jnp.float32)
            total = part if total is None else total + part
        total = total.astype(jnp.bfloat16)
        for half in range(2):
            x_ref[pl.ds(target, count), 2 * frame + half] = total[:, half * depth : (half + 1) * depth].reshape(
                count, width, depth
            )


def lift_own(own_ref, time_ref, out_ref):
    first, second = own_ref[0, 0], own_ref[0, 1]
    out_ref[0] = jnp.dot(first, time_ref[2], preferred_element_type=jnp.float32)
    out_ref[1] = jnp.dot(first, time_ref[1], preferred_element_type=jnp.float32) + jnp.dot(
        second, time_ref[2], preferred_element_type=jnp.float32
    )


def stage_kernel(plan, *refs):
    refs = list(refs)
    sources = [refs.pop(0) for _ in range(plan["sources"])]
    w_ref = refs.pop(0)
    time_ref = refs.pop(0) if plan["lifts"] else None
    for _ in range(plan["unread"]):
        refs.pop(0)
    outs = [refs.pop(0) for _ in range(plan["outs"])]
    x_ref, act_ref = [refs.pop(0) for _ in range(2)]
    frames = x_ref.shape[1]

    fetched = plan["fetched"]
    if fetched:
        in_sem = refs.pop(0)
        for source, start, count, target in plan["loads"]:
            for row in range(count):
                for frame in range(frames):
                    pltpu.make_async_copy(
                        sources[source].at[frame, start + row], x_ref.at[target + row, frame], in_sem.at[target + row]
                    ).start()
    weights = []
    if plan["fetch"]:
        w_hbm = w_ref
        w_ref, w_sem = [refs.pop(0) for _ in range(2)]
        depth = x_ref.shape[3]
        weights = [
            pltpu.make_async_copy(
                w_hbm.at[tap, pl.ds(column * depth, depth)],
                w_ref.at[tap, pl.ds(column * depth, depth)],
                w_sem.at[3 * tap + column],
            )
            for tap in range(3)
            for column in range(3)
        ]
    edges = []
    if plan["edges"]:
        edge_sem = refs.pop(0)
        edges = [
            pltpu.make_async_copy(
                sources[0].at[:, pl.ds(row, 1)], outs[plan["outs"] - len(plan["edges"]) + number], edge_sem.at[number]
            )
            for number, row in enumerate(plan["edges"])
        ]
    for copy in weights[:3] + edges:
        copy.start()
    if plan["staged"]:
        stage_ref, out_sem = [refs.pop(0) for _ in range(2)]

    for own, before, start, count, target in plan["lifts"]:
        step = min(count, 2)

        def body(number, carry, own=own, before=before, start=start, target=target, step=step):
            lift(
                sources[own], sources[before], time_ref, x_ref, start + number * step, target + number * step, step
            )
            return carry

        lax.fori_loop(0, count // step, body, 0)
    if not fetched:
        for source, start, count, target in plan["loads"]:
            x_ref[pl.ds(target, count)] = sources[source][pl.ds(start, count)]
    for out, row, count in plan["keeps"]:
        outs[out][...] = x_ref[pl.ds(row, count)]

    def prepare(row, frame):
        if fetched and frame == 0:
            pltpu.make_async_copy(x_ref.at[row], x_ref.at[row], in_sem.at[row]).wait()
        activate(x_ref, act_ref, row, frame)

    def partial_sums():
        size = frames * x_ref.shape[2]
        for row in plan["prepared"]:
            for frame in range(frames):
                prepare(row, frame)
        for out, index, residual, taps in plan["partials"]:
            total = None
            for tap, row in taps:
                lhs = act_ref[row].reshape(size, 3 * x_ref.shape[3])
                part = jnp.dot(lhs, w_ref[tap], preferred_element_type=jnp.float32)
                total = part if total is None else total + part
            if residual is not None:
                total += x_ref[residual].reshape(size, x_ref.shape[3]).astype(jnp.float32)
            outs[out][index] = total.reshape(x_ref.shape[1:])
        if plan["own_part"] is not None:
            source, out = plan["own_part"]
            lift_own(sources[source], time_ref, outs[out])

    target = 0
    for number, (source, count, active, out, start) in enumerate(plan["runs"]):
        group = min(count, 2)
        steps = count // group

        def body(step, carry, first, last, source=source, target=target, group=group, out=out, start=start):
            def between(tap):
                if first:
                    for row in range(0, group) if tap == 0 else range(group + tap - 1, group + tap):
                        if row >= active:
                            for frame in range(frames):
                                prepare(source + row, frame)
                if first and tap == 0 and number == 0:
                    for copy in weights[3:6]:
                        copy.start()
                if last:
                    return
                for at, (row, frame) in enumerate((r, f) for r in range(group) for f in range(frames)):
                    if at * 3 // (group * frames) == tap:
                        prepare(source + (step + 1) * group + 2 + row, frame)

            row = target + step * group if plan["staged"] else start + step * group
            to_ref = stage_ref if plan["staged"] else outs[out]
            parts = weights if weights and number == 0 and first else None
            convolve(x_ref, act_ref, w_ref, to_ref, source + step * group, row, group, between, parts)
            if plan["staged"]:
                for frame in range(frames):
                    pltpu.make_async_copy(
                        stage_ref.at[pl.ds(row, group), frame],
                        outs[out].at[frame, pl.ds(start + step * group, group)],
                        out_sem.at[0],
                    ).start()
            return carry

        body(0, 0, first=True, last=steps == 1)
        if steps > 2:
            lax.fori_loop(1, steps - 1, functools.partial(body, first=False, last=False), 0)
        if steps > 1:
            body(steps - 1, 0, first=False, last=True)
        target += count

    partial_sums()
    if plan["staged"]:
        pltpu.make_async_copy(stage_ref, stage_ref, out_sem.at[0]).wait()
    for copy in edges:
        copy.wait()


def stage(
    name,
    sources,
    weight,
    loads,
    runs,
    out_shapes,
    dims,
    fetched=False,
    staged=False,
    lifts=(),
    time=None,
    keeps=(),
    into=None,
    after=(),
    edges=(),
    fetch=False,
    prepared=(),
    partials=(),
    own_part=None,
):
    frames, width, channels = dims
    rows_in = max(target + count for *_, count, target in list(loads) + list(lifts))
    rows_out = sum(run[1] for run in runs)
    args = list(sources) + [weight]
    spaces = [pl.ANY if fetched else pltpu.VMEM] * len(sources) + [pltpu.HBM if fetch else pltpu.VMEM]
    if lifts:
        args.append(time)
        spaces.append(pltpu.VMEM)
    unread = list(after) + ([] if into is None else [into])
    args += unread
    spaces += [pl.ANY] * len(unread)
    out_spaces = [pltpu.HBM if staged else pltpu.VMEM] + [pltpu.VMEM] * (len(out_shapes) - 1 + len(edges))
    out_shapes = list(out_shapes) + [(frames, 1, width, channels)] * len(edges)
    plan = dict(
        sources=len(sources),
        unread=len(unread),
        outs=len(out_shapes),
        loads=loads,
        fetched=fetched,
        staged=staged,
        lifts=lifts,
        keeps=keeps,
        runs=runs,
        edges=edges,
        fetch=fetch,
        prepared=prepared,
        partials=partials,
        own_part=own_part,
    )
    in_float = {entry[0] for entry in partials} | ({own_part[1]} if own_part else set())
    scratch = [
        pltpu.VMEM((rows_in, frames, width, channels), jnp.bfloat16),
        pltpu.VMEM((rows_in, frames, width, 3 * channels), jnp.bfloat16),
    ]
    held = 2 * frames * width * channels * 4 * rows_in
    flops = 2 * rows_out * frames * width * 9 * channels * channels
    if lifts:
        flops += 2 * sum(entry[3] for entry in lifts) * frames * width * 3 * time.shape[1] * channels
    if fetched:
        scratch.append(pltpu.SemaphoreType.DMA((rows_in,)))
    if fetch:
        scratch += [pltpu.VMEM(weight.shape, jnp.bfloat16), pltpu.SemaphoreType.DMA((9,))]
        held += 2 * weight.size
    if edges:
        scratch.append(pltpu.SemaphoreType.DMA((len(edges),)))
    if staged:
        scratch += [pltpu.VMEM((rows_out, frames, width, channels), jnp.bfloat16), pltpu.SemaphoreType.DMA((1,))]
        held += 2 * frames * width * channels * rows_out
    return pl.pallas_call(
        functools.partial(stage_kernel, plan),
        out_shape=[
            jax.ShapeDtypeStruct(shape, jnp.float32 if number in in_float else jnp.bfloat16)
            for number, shape in enumerate(out_shapes)
        ],
        in_specs=[pl.BlockSpec(memory_space=space) for space in spaces],
        out_specs=[pl.BlockSpec(memory_space=space) for space in out_spaces],
        scratch_shapes=scratch,
        input_output_aliases={} if into is None else {len(args) - 1: 0},
        compiler_params=pltpu.CompilerParams(vmem_limit_bytes=held + 12 * MIB),
        cost_estimate=pl.CostEstimate(flops=flops, bytes_accessed=1024, transcendentals=0),
        name=name,
    )(*args)


def finish_kernel(pair_ref, own_ref, part_ref, time_ref, w_ref, _, out_ref, x_ref, act_ref, stage_ref, sem, *, start):
    frames, width, channels = x_ref.shape[1:]
    before, latest = pair_ref[0, 0], pair_ref[0, 1]
    for pair in range(2):
        total = own_ref[pair]
        if pair == 0:
            total += jnp.dot(before, time_ref[0], preferred_element_type=jnp.float32)
            total += jnp.dot(latest, time_ref[1], preferred_element_type=jnp.float32)
        else:
            total += jnp.dot(latest, time_ref[0], preferred_element_type=jnp.float32)
        total = total.astype(jnp.bfloat16)
        for half in range(2):
            x_ref[0, 2 * pair + half] = total[:, half * channels : (half + 1) * channels]
            activate(x_ref, act_ref, 0, 2 * pair + half)
    copies = []
    for row in range(3):
        total = jnp.dot(
            act_ref[0].reshape(frames * width, 3 * channels), w_ref[2 - row], preferred_element_type=jnp.float32
        ).reshape(frames, width, channels)
        total += part_ref[row]
        if row == 1:
            total += x_ref[0].astype(jnp.float32)
        stage_ref[row] = total.astype(jnp.bfloat16)
        copies.append(pltpu.make_async_copy(stage_ref.at[row], out_ref.at[:, start + row], sem.at[row]))
        copies[-1].start()
    for copy in copies:
        copy.wait()


def finish(name, pair, own, part, time, weight, into, start):
    rows, frames, width, channels = part.shape
    return pl.pallas_call(
        functools.partial(finish_kernel, start=start),
        out_shape=jax.ShapeDtypeStruct(into.shape, into.dtype),
        in_specs=[pl.BlockSpec(memory_space=pltpu.VMEM)] * 5 + [pl.BlockSpec(memory_space=pl.ANY)],
        out_specs=pl.BlockSpec(memory_space=pltpu.HBM),
        scratch_shapes=[
            pltpu.VMEM((1, frames, width, channels), jnp.bfloat16),
            pltpu.VMEM((1, frames, width, 3 * channels), jnp.bfloat16),
            pltpu.VMEM((rows, frames, width, channels), jnp.bfloat16),
            pltpu.SemaphoreType.DMA((rows,)),
        ],
        input_output_aliases={5: 0},
        compiler_params=pltpu.CompilerParams(vmem_limit_bytes=12 * MIB),
        cost_estimate=pl.CostEstimate(
            flops=2 * frames * width * channels * (9 * channels + 2 * time.shape[1]), bytes_accessed=1024, transcendentals=0
        ),
        name=name,
    )(pair, own, part, time, weight, into)


def to_next(value, axis):
    count = lax.axis_size(axis)
    return lax.ppermute(value, axis, [(i, i + 1) for i in range(count - 1)])


def to_previous(value, axis):
    count = lax.axis_size(axis)
    return lax.ppermute(value, axis, [(i + 1, i) for i in range(count - 1)])


def on_device(frames, space_weight, time_weight, out_weight):
    count, rows, width, channels = frames.shape
    depth = time_weight.shape[3]
    space = space_weight.reshape(3, 3 * channels, channels)
    time = time_weight.reshape(3, channels, 2 * depth)
    out_w = out_weight.reshape(3, 3 * depth, depth)
    wide = (count, width, channels)
    fine = (2 * count, width, depth)
    last = rows - 1

    def chunk(n):
        return (n, count, width, channels)

    def lifted(n):
        return (n, 2 * count, width, depth)

    here = pltpu.with_memory_space_constraint(frames, pltpu.HBM)
    space_here = pltpu.with_memory_space_constraint(space, pltpu.HBM)
    (ha,) = stage(
        "hidden_1_2", [here], space_here, [(0, 0, 4, 0)], [(0, 2, 0, 0, 0)], [chunk(2)], wide, fetched=True, fetch=True
    )
    pa = to_next(ha, "tm")
    (hb,) = stage(
        "hidden_3_6",
        [here],
        space,
        [(0, 2, 6, 0)],
        [(0, 4, 0, 0, 0)],
        [chunk(4)],
        wide,
        fetched=True,
        after=[ha],
    )
    pb = to_next(hb, "tm")
    hc, first_row, last_row = stage(
        "hidden_7_10",
        [here],
        space,
        [(0, 6, 6, 0)],
        [(0, 4, 0, 0, 0)],
        [chunk(4)],
        wide,
        fetched=True,
        after=[hb],
        edges=(0, last),
    )
    pc = to_next(hc, "tm")
    above = to_next(last_row, "rows")
    below = to_previous(first_row, "rows")
    hd, he, hf = stage(
        "hidden_rest",
        [here, above, below],
        space,
        [(1, 0, 1, 0), (0, 0, 2, 1), (0, 10, 6, 3), (2, 0, 1, 9)],
        [(0, 1, 0, 0, 1), (3, 2, 0, 1, 0), (5, 1, 2, 2, 0), (6, 1, 2, 1, 2), (7, 1, 2, 0, 0)],
        [chunk(2), chunk(3), chunk(1)],
        wide,
        fetched=True,
        after=[hc, pa],
    )
    pd = to_next(hd, "tm")
    pe = to_next(he, "tm")
    pf = to_next(hf, "tm")

    whole = (2 * count, rows, width, depth)
    out, ua, ub = stage(
        "out_2_5",
        [ha, pa, hb, pb],
        out_w,
        [],
        [(0, 4, 0, 0, 2)],
        [whole, lifted(2), lifted(2)],
        fine,
        staged=True,
        lifts=[(0, 1, 0, 2, 0), (2, 3, 0, 4, 2)],
        time=time,
        keeps=[(1, 0, 2), (2, 4, 2)],
        after=[hd],
    )
    out, uc = stage(
        "out_6_9",
        [hc, pc, ub],
        out_w,
        [(2, 0, 2, 0)],
        [(0, 4, 0, 0, 6)],
        [whole, lifted(2)],
        fine,
        staged=True,
        lifts=[(0, 1, 0, 4, 2)],
        time=time,
        keeps=[(1, 4, 2)],
        into=out,
    )
    ud = upsample("up_edges", hd, pd, time, depth, uc)
    up_above = to_next(ud[:1], "rows")
    up_below = to_previous(ud[1:], "rows")
    (out,) = stage(
        "out_0_1",
        [ua, ud, up_above],
        out_w,
        [(2, 0, 1, 0), (1, 1, 1, 1), (0, 0, 2, 2)],
        [(0, 2, 0, 0, 0)],
        [whole],
        fine,
        staged=True,
        into=out,
    )
    out, part, own_part = stage(
        "out_10_15",
        [he, pe, uc, ud, up_below, hf],
        out_w,
        [(2, 0, 2, 0), (3, 0, 1, 5), (4, 0, 1, 6)],
        [(0, 2, 0, 0, 10), (4, 1, 0, 0, 15)],
        [whole, (3,) + lifted(1)[1:], (2, width, 2 * depth)],
        fine,
        staged=True,
        lifts=[(0, 1, 0, 2, 2), (0, 1, 2, 1, 4)],
        time=time,
        into=out,
        partials=[
            (1, 0, 3, ((0, 2), (1, 3))),
            (1, 1, None, ((0, 3), (2, 4))),
            (1, 2, 4, ((1, 4), (2, 5))),
        ],
        own_part=(5, 2),
    )
    return finish("out_12_14", pf, own_part, part, time, out_w, out, 12)


def upsample_kernel(own_ref, prev_ref, w_ref, _, out_ref):
    rows, _, width, channels = own_ref.shape
    depth = out_ref.shape[3]
    size = rows * width
    window = [
        prev_ref[:, 0].reshape(size, channels),
        prev_ref[:, 1].reshape(size, channels),
        own_ref[:, 0].reshape(size, channels),
        own_ref[:, 1].reshape(size, channels),
    ]
    for frame in range(2):
        total = jnp.dot(window[frame], w_ref[0], preferred_element_type=jnp.float32)
        for tap in (1, 2):
            total += jnp.dot(window[frame + tap], w_ref[tap], preferred_element_type=jnp.float32)
        total = total.astype(jnp.bfloat16)
        for half in range(2):
            out_ref[:, 2 * frame + half] = total[:, half * depth : (half + 1) * depth].reshape(
                rows, width, depth
            )


def upsample(name, own, prev, weight, depth, after):
    rows, frames, width, channels = own.shape
    return pl.pallas_call(
        upsample_kernel,
        out_shape=jax.ShapeDtypeStruct((rows, 2 * frames, width, depth), jnp.bfloat16),
        in_specs=[pl.BlockSpec(memory_space=pltpu.VMEM)] * 3 + [pl.BlockSpec(memory_space=pltpu.HBM)],
        out_specs=pl.BlockSpec(memory_space=pltpu.VMEM),
        compiler_params=pltpu.CompilerParams(vmem_limit_bytes=12 * MIB),
        cost_estimate=pl.CostEstimate(
            flops=2 * rows * frames * width * 3 * channels * 2 * depth,
            bytes_accessed=2 * rows * frames * width * (2 * channels + 2 * depth) + 2 * weight.size,
            transcendentals=0,
        ),
        name=name,
    )(own, prev, weight, after)


def solution(mesh):
    return jax.shard_map(
        on_device,
        mesh=mesh,
        in_specs=(P("tm", "rows", None, None), P(), P(), P()),
        out_specs=P("tm", "rows", None, None),
        check_vma=False,
    )
```

```python
import functools

import jax
import jax.numpy as jnp
from jax import lax
from jax.experimental import pallas as pl
from jax.experimental.pallas import tpu as pltpu
from jax.sharding import PartitionSpec as P

MIB = 1024 * 1024


def silu(v):
    half = 0.5 * v
    return half + half * jnp.tanh(half)


def activate(x_ref, act_ref, row, frame):
    width, channels = x_ref.shape[2:]
    step = 256
    column = lax.broadcasted_iota(jnp.int32, (width, step), 0)
    for start in range(0, channels, step):
        v = x_ref[row, frame, :, start : start + step].astype(jnp.float32)
        a = silu(v)
        before = jnp.where(column == 0, 0.0, pltpu.roll(a, 1, 0))
        after = jnp.where(column == width - 1, 0.0, pltpu.roll(a, width - 1, 0))
        for tap, value in enumerate((before, a, after)):
            act_ref[row, frame, :, tap * channels + start : tap * channels + start + step] = value.astype(
                jnp.bfloat16
            )


def convolve(x_ref, act_ref, w_ref, out_ref, source, target, group, between, parts=None):
    _, frames, width, channels = x_ref.shape
    size = group * frames * width
    total = None
    for tap in range(3):
        between(tap)
        if parts is None:
            lhs = act_ref[pl.ds(source + tap, group)].reshape(size, 3 * channels)
            part = jnp.dot(lhs, w_ref[tap], preferred_element_type=jnp.float32)
            total = part if total is None else total + part
            continue
        for column in range(3):
            parts[3 * tap + column].wait()
            if tap == 0 and column == 2:
                for copy in parts[6:]:
                    copy.start()
            span = slice(column * channels, (column + 1) * channels)
            lhs = act_ref[pl.ds(source + tap, group), :, :, span].reshape(size, channels)
            part = jnp.dot(lhs, w_ref[tap, span], preferred_element_type=jnp.float32)
            total = part if total is None else total + part
    total += x_ref[pl.ds(source + 1, group)].reshape(size, channels).astype(jnp.float32)
    out_ref[pl.ds(target, group)] = total.astype(jnp.bfloat16).reshape(group, frames, width, channels)


def lift(own_ref, before_ref, time_ref, x_ref, source, target, count):
    _, frames, width, channels = own_ref.shape
    depth = x_ref.shape[3]
    size = count * width
    window = [
        ref[pl.ds(source, count), frame].reshape(size, channels)
        for ref in (before_ref, own_ref)
        for frame in range(frames)
    ]
    for frame in range(frames):
        total = None
        for tap in range(3):
            part = jnp.dot(window[frame + tap], time_ref[tap], preferred_element_type=jnp.float32)
            total = part if total is None else total + part
        total = total.astype(jnp.bfloat16)
        for half in range(2):
            x_ref[pl.ds(target, count), 2 * frame + half] = total[:, half * depth : (half + 1) * depth].reshape(
                count, width, depth
            )


def lift_own(own_ref, start, count, time_ref, out_ref, at):
    _, _, width, channels = own_ref.shape
    size = count * width
    first, second = [own_ref[start : start + count, frame].reshape(size, channels) for frame in range(2)]
    shape = (count,) + out_ref.shape[2:]
    total = jnp.dot(first, time_ref[2], preferred_element_type=jnp.float32)
    out_ref[at : at + count, 0] = total.reshape(shape)
    total = jnp.dot(first, time_ref[1], preferred_element_type=jnp.float32)
    total += jnp.dot(second, time_ref[2], preferred_element_type=jnp.float32)
    out_ref[at : at + count, 1] = total.reshape(shape)


def stage_kernel(plan, *refs):
    refs = list(refs)
    sources = [refs.pop(0) for _ in range(plan["sources"])]
    w_ref = refs.pop(0)
    time_ref = refs.pop(0) if plan["lifts"] or plan["own_parts"] else None
    for _ in range(plan["unread"]):
        refs.pop(0)
    outs = [refs.pop(0) for _ in range(plan["outs"])]
    x_ref, act_ref = [refs.pop(0) for _ in range(2)]
    frames = x_ref.shape[1]

    fetched = plan["fetched"]
    if fetched:
        in_sem = refs.pop(0)
        for source, start, count, target in plan["loads"]:
            for row in range(count):
                for frame in range(frames):
                    pltpu.make_async_copy(
                        sources[source].at[frame, start + row], x_ref.at[target + row, frame], in_sem.at[target + row]
                    ).start()
    weights = []
    if plan["fetch"]:
        w_hbm = w_ref
        w_ref, w_sem = [refs.pop(0) for _ in range(2)]
        depth = x_ref.shape[3]
        weights = [
            pltpu.make_async_copy(
                w_hbm.at[tap, pl.ds(column * depth, depth)],
                w_ref.at[tap, pl.ds(column * depth, depth)],
                w_sem.at[3 * tap + column],
            )
            for tap in range(3)
            for column in range(3)
        ]
    edges = []
    if plan["edges"]:
        edge_sem = refs.pop(0)
        edges = [
            pltpu.make_async_copy(
                sources[0].at[:, pl.ds(row, 1)], outs[plan["outs"] - len(plan["edges"]) + number], edge_sem.at[number]
            )
            for number, row in enumerate(plan["edges"])
        ]
    for copy in weights[:3] + edges:
        copy.start()
    if plan["staged"]:
        stage_ref, out_sem = [refs.pop(0) for _ in range(2)]

    for own, before, start, count, target in plan["lifts"]:
        step = min(count, 2)

        def body(number, carry, own=own, before=before, start=start, target=target, step=step):
            lift(
                sources[own], sources[before], time_ref, x_ref, start + number * step, target + number * step, step
            )
            return carry

        lax.fori_loop(0, count // step, body, 0)
    if not fetched:
        for source, start, count, target in plan["loads"]:
            x_ref[pl.ds(target, count)] = sources[source][pl.ds(start, count)]
    for out, row, count in plan["keeps"]:
        outs[out][...] = x_ref[pl.ds(row, count)]

    def prepare(row, frame):
        if fetched and frame == 0:
            pltpu.make_async_copy(x_ref.at[row], x_ref.at[row], in_sem.at[row]).wait()
        activate(x_ref, act_ref, row, frame)

    def partial_sums():
        size = frames * x_ref.shape[2]
        for row in plan["prepared"]:
            for frame in range(frames):
                prepare(row, frame)
        for out, index, residual, taps in plan["partials"]:
            total = None
            for tap, row in taps:
                lhs = act_ref[row].reshape(size, 3 * x_ref.shape[3])
                part = jnp.dot(lhs, w_ref[tap], preferred_element_type=jnp.float32)
                total = part if total is None else total + part
            if residual is not None:
                total += x_ref[residual].reshape(size, x_ref.shape[3]).astype(jnp.float32)
            outs[out][index] = total.reshape(x_ref.shape[1:])
        for source, start, count, out, at in plan["own_parts"]:
            lift_own(sources[source], start, count, time_ref, outs[out], at)

    target = 0
    for number, (source, count, active, out, start) in enumerate(plan["runs"]):
        group = min(count, 2)
        steps = count // group

        def body(step, carry, first, last, source=source, target=target, group=group, out=out, start=start):
            def between(tap):
                if first:
                    for row in range(0, group) if tap == 0 else range(group + tap - 1, group + tap):
                        if row >= active:
                            for frame in range(frames):
                                prepare(source + row, frame)
                if first and tap == 0 and number == 0:
                    for copy in weights[3:6]:
                        copy.start()
                if last:
                    return
                for at, (row, frame) in enumerate((r, f) for r in range(group) for f in range(frames)):
                    if at * 3 // (group * frames) == tap:
                        prepare(source + (step + 1) * group + 2 + row, frame)

            row = target + step * group if plan["staged"] else start + step * group
            to_ref = stage_ref if plan["staged"] else outs[out]
            parts = weights if weights and number == 0 and first else None
            convolve(x_ref, act_ref, w_ref, to_ref, source + step * group, row, group, between, parts)
            if plan["staged"]:
                for frame in range(frames):
                    pltpu.make_async_copy(
                        stage_ref.at[pl.ds(row, group), frame],
                        outs[out].at[frame, pl.ds(start + step * group, group)],
                        out_sem.at[0],
                    ).start()
            return carry

        body(0, 0, first=True, last=steps == 1)
        if steps > 2:
            lax.fori_loop(1, steps - 1, functools.partial(body, first=False, last=False), 0)
        if steps > 1:
            body(steps - 1, 0, first=False, last=True)
        target += count

    partial_sums()
    if plan["staged"]:
        pltpu.make_async_copy(stage_ref, stage_ref, out_sem.at[0]).wait()
    for copy in edges:
        copy.wait()


def stage(
    name,
    sources,
    weight,
    loads,
    runs,
    out_shapes,
    dims,
    fetched=False,
    staged=False,
    lifts=(),
    time=None,
    keeps=(),
    into=None,
    after=(),
    edges=(),
    fetch=False,
    prepared=(),
    partials=(),
    own_parts=(),
):
    frames, width, channels = dims
    rows_in = max(target + count for *_, count, target in list(loads) + list(lifts))
    rows_out = sum(run[1] for run in runs)
    args = list(sources) + [weight]
    spaces = [pl.ANY if fetched else pltpu.VMEM] * len(sources) + [pltpu.HBM if fetch else pltpu.VMEM]
    if lifts or own_parts:
        args.append(time)
        spaces.append(pltpu.VMEM)
    unread = list(after) + ([] if into is None else [into])
    args += unread
    spaces += [pl.ANY] * len(unread)
    out_spaces = [pltpu.HBM if staged else pltpu.VMEM] + [pltpu.VMEM] * (len(out_shapes) - 1 + len(edges))
    out_shapes = list(out_shapes) + [(frames, 1, width, channels)] * len(edges)
    plan = dict(
        sources=len(sources),
        unread=len(unread),
        outs=len(out_shapes),
        loads=loads,
        fetched=fetched,
        staged=staged,
        lifts=lifts,
        keeps=keeps,
        runs=runs,
        edges=edges,
        fetch=fetch,
        prepared=prepared,
        partials=partials,
        own_parts=own_parts,
    )
    in_float = {entry[0] for entry in partials} | {entry[3] for entry in own_parts}
    scratch = [
        pltpu.VMEM((rows_in, frames, width, channels), jnp.bfloat16),
        pltpu.VMEM((rows_in, frames, width, 3 * channels), jnp.bfloat16),
    ]
    held = 2 * frames * width * channels * 4 * rows_in
    flops = 2 * rows_out * frames * width * 9 * channels * channels
    if lifts:
        flops += 2 * sum(entry[3] for entry in lifts) * frames * width * 3 * time.shape[1] * channels
    if fetched:
        scratch.append(pltpu.SemaphoreType.DMA((rows_in,)))
    if fetch:
        scratch += [pltpu.VMEM(weight.shape, jnp.bfloat16), pltpu.SemaphoreType.DMA((9,))]
        held += 2 * weight.size
    if edges:
        scratch.append(pltpu.SemaphoreType.DMA((len(edges),)))
    if staged:
        scratch += [pltpu.VMEM((rows_out, frames, width, channels), jnp.bfloat16), pltpu.SemaphoreType.DMA((1,))]
        held += 2 * frames * width * channels * rows_out
    return pl.pallas_call(
        functools.partial(stage_kernel, plan),
        out_shape=[
            jax.ShapeDtypeStruct(shape, jnp.float32 if number in in_float else jnp.bfloat16)
            for number, shape in enumerate(out_shapes)
        ],
        in_specs=[pl.BlockSpec(memory_space=space) for space in spaces],
        out_specs=[pl.BlockSpec(memory_space=space) for space in out_spaces],
        scratch_shapes=scratch,
        input_output_aliases={} if into is None else {len(args) - 1: 0},
        compiler_params=pltpu.CompilerParams(vmem_limit_bytes=held + 12 * MIB),
        cost_estimate=pl.CostEstimate(flops=flops, bytes_accessed=1024, transcendentals=0),
        name=name,
    )(*args)


def arrive_kernel(plan, *refs):
    pair_ref, own_ref, part_ref, time_ref, w_ref, _, out_ref = refs[:7]
    refs = list(refs[7:])
    later_ref = refs.pop(0) if plan["later"] else None
    x_ref, act_ref, stage_ref, sem = refs
    count, frames, width, channels = x_ref.shape
    depth = pair_ref.shape[3]
    before, latest = [pair_ref[:, frame].reshape(count * width, depth) for frame in range(2)]
    for pair in range(2):
        total = own_ref[plan["own_at"] : plan["own_at"] + count, pair].reshape(count * width, 2 * channels)
        if pair == 0:
            total += jnp.dot(before, time_ref[0], preferred_element_type=jnp.float32)
            total += jnp.dot(latest, time_ref[1], preferred_element_type=jnp.float32)
        else:
            total += jnp.dot(latest, time_ref[0], preferred_element_type=jnp.float32)
        total = total.astype(jnp.bfloat16)
        for half in range(2):
            x_ref[:, 2 * pair + half] = total[:, half * channels : (half + 1) * channels].reshape(
                count, width, channels
            )
            for row in range(count):
                activate(x_ref, act_ref, row, 2 * pair + half)
    copies = []
    for later, index, part, residual, taps in plan["terms"]:
        total = None
        for tap, row in taps:
            lhs = act_ref[row].reshape(frames * width, 3 * channels)
            value = jnp.dot(lhs, w_ref[tap], preferred_element_type=jnp.float32)
            total = value if total is None else total + value
        total = total.reshape(frames, width, channels)
        if part is not None:
            total += part_ref[part]
        if residual is not None:
            total += x_ref[residual].astype(jnp.float32)
        if later:
            later_ref[index] = total
            continue
        place = len(copies)
        stage_ref[place] = total.astype(jnp.bfloat16)
        copies.append(pltpu.make_async_copy(stage_ref.at[place], out_ref.at[:, index], sem.at[place]))
        copies[-1].start()
    for copy in copies:
        copy.wait()


def arrive(name, pair, own, own_at, part, time, weight, into, terms):
    count = pair.shape[0]
    _, frames, width, channels = part.shape
    later = sum(term[0] for term in terms)
    final = len(terms) - later
    shapes = [jax.ShapeDtypeStruct(into.shape, into.dtype)]
    if later:
        shapes.append(jax.ShapeDtypeStruct((later,) + part.shape[1:], jnp.float32))
    return pl.pallas_call(
        functools.partial(arrive_kernel, dict(terms=terms, own_at=own_at, later=later)),
        out_shape=shapes,
        in_specs=[pl.BlockSpec(memory_space=pltpu.VMEM)] * 5 + [pl.BlockSpec(memory_space=pl.ANY)],
        out_specs=[pl.BlockSpec(memory_space=pltpu.HBM)] + [pl.BlockSpec(memory_space=pltpu.VMEM)] * (len(shapes) - 1),
        scratch_shapes=[
            pltpu.VMEM((count, frames, width, channels), jnp.bfloat16),
            pltpu.VMEM((count, frames, width, 3 * channels), jnp.bfloat16),
            pltpu.VMEM((final, frames, width, channels), jnp.bfloat16),
            pltpu.SemaphoreType.DMA((final,)),
        ],
        input_output_aliases={5: 0},
        compiler_params=pltpu.CompilerParams(vmem_limit_bytes=16 * MIB),
        cost_estimate=pl.CostEstimate(
            flops=2 * frames * width * channels * (3 * len(terms) * channels + 2 * count * time.shape[1]),
            bytes_accessed=1024,
            transcendentals=0,
        ),
        name=name,
    )(pair, own, part, time, weight, into)


def to_next(value, axis):
    count = lax.axis_size(axis)
    return lax.ppermute(value, axis, [(i, i + 1) for i in range(count - 1)])


def to_previous(value, axis):
    count = lax.axis_size(axis)
    return lax.ppermute(value, axis, [(i + 1, i) for i in range(count - 1)])


def on_device(frames, space_weight, time_weight, out_weight):
    count, rows, width, channels = frames.shape
    depth = time_weight.shape[3]
    space = space_weight.reshape(3, 3 * channels, channels)
    time = time_weight.reshape(3, channels, 2 * depth)
    out_w = out_weight.reshape(3, 3 * depth, depth)
    wide = (count, width, channels)
    fine = (2 * count, width, depth)
    last = rows - 1

    def chunk(n):
        return (n, count, width, channels)

    def lifted(n):
        return (n, 2 * count, width, depth)

    here = pltpu.with_memory_space_constraint(frames, pltpu.HBM)
    space_here = pltpu.with_memory_space_constraint(space, pltpu.HBM)
    (ha,) = stage(
        "hidden_1_2", [here], space_here, [(0, 0, 4, 0)], [(0, 2, 0, 0, 0)], [chunk(2)], wide, fetched=True, fetch=True
    )
    pa = to_next(ha, "tm")
    (hb,) = stage(
        "hidden_3_6",
        [here],
        space,
        [(0, 2, 6, 0)],
        [(0, 4, 0, 0, 0)],
        [chunk(4)],
        wide,
        fetched=True,
        after=[ha],
    )
    pb = to_next(hb, "tm")
    hc, first_row, last_row = stage(
        "hidden_7_10",
        [here],
        space,
        [(0, 6, 6, 0)],
        [(0, 4, 0, 0, 0)],
        [chunk(4)],
        wide,
        fetched=True,
        after=[hb],
        edges=(0, last),
    )
    pc = to_next(hc, "tm")
    above = to_next(last_row, "rows")
    below = to_previous(first_row, "rows")
    hd, he, hf = stage(
        "hidden_rest",
        [here, above, below],
        space,
        [(1, 0, 1, 0), (0, 0, 2, 1), (0, 10, 6, 3), (2, 0, 1, 9)],
        [(0, 1, 0, 0, 1), (3, 2, 0, 1, 0), (5, 1, 2, 2, 0), (6, 1, 2, 1, 2), (7, 1, 2, 0, 0)],
        [chunk(2), chunk(3), chunk(1)],
        wide,
        fetched=True,
        after=[hc, pa],
    )
    pd = to_next(hd, "tm")
    pe = to_next(he, "tm")
    pf = to_next(hf, "tm")

    whole = (2 * count, rows, width, depth)
    out, ua, ub = stage(
        "out_2_5",
        [ha, pa, hb, pb],
        out_w,
        [],
        [(0, 4, 0, 0, 2)],
        [whole, lifted(2), lifted(2)],
        fine,
        staged=True,
        lifts=[(0, 1, 0, 2, 0), (2, 3, 0, 4, 2)],
        time=time,
        keeps=[(1, 0, 2), (2, 4, 2)],
        after=[hd],
    )
    out, uc = stage(
        "out_6_9",
        [hc, pc, ub],
        out_w,
        [(2, 0, 2, 0)],
        [(0, 4, 0, 0, 6)],
        [whole, lifted(2)],
        fine,
        staged=True,
        lifts=[(0, 1, 0, 4, 2)],
        time=time,
        keeps=[(1, 4, 2)],
        into=out,
    )
    ud = upsample("up_edges", hd, pd, time, depth, uc)
    up_above = to_next(ud[:1], "rows")
    up_below = to_previous(ud[1:], "rows")
    out, part, own = stage(
        "out_0_1",
        [ua, ud, up_above, uc, up_below, he, hf],
        out_w,
        [(2, 0, 1, 0), (1, 1, 1, 1), (0, 0, 2, 2), (3, 0, 2, 4), (1, 0, 1, 6), (4, 0, 1, 7)],
        [(0, 2, 0, 0, 0)],
        [whole, (4,) + lifted(1)[1:], (4, 2, width, 2 * depth)],
        fine,
        staged=True,
        into=out,
        time=time,
        prepared=(4, 5, 6, 7),
        partials=[
            (1, 0, 5, ((0, 4), (1, 5))),
            (1, 1, None, ((0, 5),)),
            (1, 2, None, ((2, 6),)),
            (1, 3, 6, ((1, 6), (2, 7))),
        ],
        own_parts=[(5, 0, 3, 2, 0), (6, 0, 1, 2, 3)],
    )
    out, last_part = arrive(
        "out_10_15",
        pe,
        own,
        0,
        part,
        time,
        out_w,
        out,
        [
            (False, 10, 0, None, ((2, 0),)),
            (False, 11, 1, 0, ((1, 0), (2, 1))),
            (False, 15, 3, None, ((0, 2),)),
            (True, 0, None, 1, ((0, 0), (1, 1))),
            (True, 1, None, None, ((0, 1), (2, 2))),
            (True, 2, 2, 2, ((1, 2),)),
        ],
    )
    (out,) = arrive(
        "out_12_14",
        pf,
        own,
        3,
        last_part,
        time,
        out_w,
        out,
        [
            (False, 12, 0, None, ((2, 0),)),
            (False, 13, 1, 0, ((1, 0),)),
            (False, 14, 2, None, ((0, 0),)),
        ],
    )
    return out


def upsample_kernel(own_ref, prev_ref, w_ref, _, out_ref):
    rows, _, width, channels = own_ref.shape
    depth = out_ref.shape[3]
    size = rows * width
    window = [
        prev_ref[:, 0].reshape(size, channels),
        prev_ref[:, 1].reshape(size, channels),
        own_ref[:, 0].reshape(size, channels),
        own_ref[:, 1].reshape(size, channels),
    ]
    for frame in range(2):
        total = jnp.dot(window[frame], w_ref[0], preferred_element_type=jnp.float32)
        for tap in (1, 2):
            total += jnp.dot(window[frame + tap], w_ref[tap], preferred_element_type=jnp.float32)
        total = total.astype(jnp.bfloat16)
        for half in range(2):
            out_ref[:, 2 * frame + half] = total[:, half * depth : (half + 1) * depth].reshape(
                rows, width, depth
            )


def upsample(name, own, prev, weight, depth, after):
    rows, frames, width, channels = own.shape
    return pl.pallas_call(
        upsample_kernel,
        out_shape=jax.ShapeDtypeStruct((rows, 2 * frames, width, depth), jnp.bfloat16),
        in_specs=[pl.BlockSpec(memory_space=pltpu.VMEM)] * 3 + [pl.BlockSpec(memory_space=pltpu.HBM)],
        out_specs=pl.BlockSpec(memory_space=pltpu.VMEM),
        compiler_params=pltpu.CompilerParams(vmem_limit_bytes=12 * MIB),
        cost_estimate=pl.CostEstimate(
            flops=2 * rows * frames * width * 3 * channels * 2 * depth,
            bytes_accessed=2 * rows * frames * width * (2 * channels + 2 * depth) + 2 * weight.size,
            transcendentals=0,
        ),
        name=name,
    )(own, prev, weight, after)


def solution(mesh):
    return jax.shard_map(
        on_device,
        mesh=mesh,
        in_specs=(P("tm", "rows", None, None), P(), P(), P()),
        out_specs=P("tm", "rows", None, None),
        check_vma=False,
    )
```

```python
import functools

import jax
import jax.numpy as jnp
from jax import lax
from jax.experimental import pallas as pl
from jax.experimental.pallas import tpu as pltpu
from jax.sharding import PartitionSpec as P

MIB = 1024 * 1024


def silu(v):
    half = 0.5 * v
    return half + half * jnp.tanh(half)


def activate(x_ref, act_ref, row, frame):
    width, channels = x_ref.shape[2:]
    step = 256
    column = lax.broadcasted_iota(jnp.int32, (width, step), 0)
    for start in range(0, channels, step):
        v = x_ref[row, frame, :, start : start + step].astype(jnp.float32)
        a = silu(v)
        before = jnp.where(column == 0, 0.0, pltpu.roll(a, 1, 0))
        after = jnp.where(column == width - 1, 0.0, pltpu.roll(a, width - 1, 0))
        for tap, value in enumerate((before, a, after)):
            act_ref[row, frame, :, tap * channels + start : tap * channels + start + step] = value.astype(
                jnp.bfloat16
            )


def convolve(x_ref, act_ref, w_ref, out_ref, source, target, group, between, parts=None):
    _, frames, width, channels = x_ref.shape
    size = group * frames * width
    total = None
    for tap in range(3):
        between(tap)
        if parts is None:
            lhs = act_ref[pl.ds(source + tap, group)].reshape(size, 3 * channels)
            part = jnp.dot(lhs, w_ref[tap], preferred_element_type=jnp.float32)
            total = part if total is None else total + part
            continue
        for column in range(3):
            parts[3 * tap + column].wait()
            if tap == 0 and column == 2:
                for copy in parts[6:]:
                    copy.start()
            span = slice(column * channels, (column + 1) * channels)
            lhs = act_ref[pl.ds(source + tap, group), :, :, span].reshape(size, channels)
            part = jnp.dot(lhs, w_ref[tap, span], preferred_element_type=jnp.float32)
            total = part if total is None else total + part
    total += x_ref[pl.ds(source + 1, group)].reshape(size, channels).astype(jnp.float32)
    out_ref[pl.ds(target, group)] = total.astype(jnp.bfloat16).reshape(group, frames, width, channels)


def lift(own_ref, before_ref, time_ref, x_ref, source, target, count):
    _, frames, width, channels = own_ref.shape
    depth = x_ref.shape[3]
    size = count * width
    window = [
        ref[pl.ds(source, count), frame].reshape(size, channels)
        for ref in (before_ref, own_ref)
        for frame in range(frames)
    ]
    for frame in range(frames):
        total = None
        for tap in range(3):
            part = jnp.dot(window[frame + tap], time_ref[tap], preferred_element_type=jnp.float32)
            total = part if total is None else total + part
        total = total.astype(jnp.bfloat16)
        for half in range(2):
            x_ref[pl.ds(target, count), 2 * frame + half] = total[:, half * depth : (half + 1) * depth].reshape(
                count, width, depth
            )


def lift_own(own_ref, start, count, time_ref, out_ref, at):
    _, _, width, channels = own_ref.shape
    size = count * width
    first, second = [own_ref[start : start + count, frame].reshape(size, channels) for frame in range(2)]
    shape = (count,) + out_ref.shape[2:]
    total = jnp.dot(first, time_ref[2], preferred_element_type=jnp.float32)
    out_ref[at : at + count, 0] = total.reshape(shape)
    total = jnp.dot(first, time_ref[1], preferred_element_type=jnp.float32)
    total += jnp.dot(second, time_ref[2], preferred_element_type=jnp.float32)
    out_ref[at : at + count, 1] = total.reshape(shape)


def stage_kernel(plan, *refs):
    refs = list(refs)
    sources = [refs.pop(0) for _ in range(plan["sources"])]
    w_ref = refs.pop(0)
    time_ref = refs.pop(0) if plan["lifts"] or plan["own_parts"] else None
    for _ in range(plan["unread"]):
        refs.pop(0)
    outs = [refs.pop(0) for _ in range(plan["outs"])]
    x_ref, act_ref = [refs.pop(0) for _ in range(2)]
    frames = x_ref.shape[1]

    fetched = plan["fetched"]
    if fetched:
        in_sem = refs.pop(0)
        for source, start, count, target in plan["loads"]:
            for row in range(count):
                for frame in range(frames):
                    pltpu.make_async_copy(
                        sources[source].at[frame, start + row], x_ref.at[target + row, frame], in_sem.at[target + row]
                    ).start()
    weights = []
    if plan["fetch"]:
        w_hbm = w_ref
        w_ref, w_sem = [refs.pop(0) for _ in range(2)]
        depth = x_ref.shape[3]
        weights = [
            pltpu.make_async_copy(
                w_hbm.at[tap, pl.ds(column * depth, depth)],
                w_ref.at[tap, pl.ds(column * depth, depth)],
                w_sem.at[3 * tap + column],
            )
            for tap in range(3)
            for column in range(3)
        ]
    edges = []
    if plan["edges"]:
        edge_sem = refs.pop(0)
        edges = [
            pltpu.make_async_copy(
                sources[0].at[:, pl.ds(row, 1)], outs[plan["outs"] - len(plan["edges"]) + number], edge_sem.at[number]
            )
            for number, row in enumerate(plan["edges"])
        ]
    for copy in weights[:3] + edges:
        copy.start()
    if plan["staged"]:
        stage_ref, out_sem = [refs.pop(0) for _ in range(2)]

    for own, before, start, count, target in plan["lifts"]:
        step = min(count, 2)

        def body(number, carry, own=own, before=before, start=start, target=target, step=step):
            lift(
                sources[own], sources[before], time_ref, x_ref, start + number * step, target + number * step, step
            )
            return carry

        lax.fori_loop(0, count // step, body, 0)
    if not fetched:
        for source, start, count, target in plan["loads"]:
            x_ref[pl.ds(target, count)] = sources[source][pl.ds(start, count)]
    for out, row, count in plan["keeps"]:
        outs[out][...] = x_ref[pl.ds(row, count)]

    def prepare(row, frame):
        if fetched and frame == 0:
            pltpu.make_async_copy(x_ref.at[row], x_ref.at[row], in_sem.at[row]).wait()
        activate(x_ref, act_ref, row, frame)

    def partial_sums():
        size = frames * x_ref.shape[2]
        for row in plan["prepared"]:
            for frame in range(frames):
                prepare(row, frame)
        for out, index, residual, taps in plan["partials"]:
            total = None
            for tap, row in taps:
                lhs = act_ref[row].reshape(size, 3 * x_ref.shape[3])
                part = jnp.dot(lhs, w_ref[tap], preferred_element_type=jnp.float32)
                total = part if total is None else total + part
            if residual is not None:
                total += x_ref[residual].reshape(size, x_ref.shape[3]).astype(jnp.float32)
            outs[out][index] = total.reshape(x_ref.shape[1:])
        for source, start, count, out, at in plan["own_parts"]:
            lift_own(sources[source], start, count, time_ref, outs[out], at)

    target = 0
    for number, (source, count, active, out, start) in enumerate(plan["runs"]):
        group = min(count, 2)
        steps = count // group

        def body(step, carry, first, last, source=source, target=target, group=group, out=out, start=start):
            def between(tap):
                if first:
                    for row in range(0, group) if tap == 0 else range(group + tap - 1, group + tap):
                        if row >= active:
                            for frame in range(frames):
                                prepare(source + row, frame)
                if first and tap == 0 and number == 0:
                    for copy in weights[3:6]:
                        copy.start()
                if last:
                    return
                for at, (row, frame) in enumerate((r, f) for r in range(group) for f in range(frames)):
                    if at * 3 // (group * frames) == tap:
                        prepare(source + (step + 1) * group + 2 + row, frame)

            row = target + step * group if plan["staged"] else start + step * group
            to_ref = stage_ref if plan["staged"] else outs[out]
            parts = weights if weights and number == 0 and first else None
            convolve(x_ref, act_ref, w_ref, to_ref, source + step * group, row, group, between, parts)
            if plan["staged"]:
                for frame in range(frames):
                    pltpu.make_async_copy(
                        stage_ref.at[pl.ds(row, group), frame],
                        outs[out].at[frame, pl.ds(start + step * group, group)],
                        out_sem.at[0],
                    ).start()
            return carry

        body(0, 0, first=True, last=steps == 1)
        if steps > 2:
            lax.fori_loop(1, steps - 1, functools.partial(body, first=False, last=False), 0)
        if steps > 1:
            body(steps - 1, 0, first=False, last=True)
        target += count

    partial_sums()
    if plan["staged"]:
        pltpu.make_async_copy(stage_ref, stage_ref, out_sem.at[0]).wait()
    for copy in edges:
        copy.wait()


def stage(
    name,
    sources,
    weight,
    loads,
    runs,
    out_shapes,
    dims,
    fetched=False,
    staged=False,
    lifts=(),
    time=None,
    keeps=(),
    into=None,
    after=(),
    edges=(),
    fetch=False,
    prepared=(),
    partials=(),
    own_parts=(),
):
    frames, width, channels = dims
    rows_in = max(target + count for *_, count, target in list(loads) + list(lifts))
    rows_out = sum(run[1] for run in runs)
    args = list(sources) + [weight]
    spaces = [pl.ANY if fetched else pltpu.VMEM] * len(sources) + [pltpu.HBM if fetch else pltpu.VMEM]
    if lifts or own_parts:
        args.append(time)
        spaces.append(pltpu.VMEM)
    unread = list(after) + ([] if into is None else [into])
    args += unread
    spaces += [pl.ANY] * len(unread)
    out_spaces = [pltpu.HBM if staged else pltpu.VMEM] + [pltpu.VMEM] * (len(out_shapes) - 1 + len(edges))
    out_shapes = list(out_shapes) + [(frames, 1, width, channels)] * len(edges)
    plan = dict(
        sources=len(sources),
        unread=len(unread),
        outs=len(out_shapes),
        loads=loads,
        fetched=fetched,
        staged=staged,
        lifts=lifts,
        keeps=keeps,
        runs=runs,
        edges=edges,
        fetch=fetch,
        prepared=prepared,
        partials=partials,
        own_parts=own_parts,
    )
    in_float = {entry[0] for entry in partials} | {entry[3] for entry in own_parts}
    scratch = [
        pltpu.VMEM((rows_in, frames, width, channels), jnp.bfloat16),
        pltpu.VMEM((rows_in, frames, width, 3 * channels), jnp.bfloat16),
    ]
    held = 2 * frames * width * channels * 4 * rows_in
    flops = 2 * rows_out * frames * width * 9 * channels * channels
    if lifts:
        flops += 2 * sum(entry[3] for entry in lifts) * frames * width * 3 * time.shape[1] * channels
    if fetched:
        scratch.append(pltpu.SemaphoreType.DMA((rows_in,)))
    if fetch:
        scratch += [pltpu.VMEM(weight.shape, jnp.bfloat16), pltpu.SemaphoreType.DMA((9,))]
        held += 2 * weight.size
    if edges:
        scratch.append(pltpu.SemaphoreType.DMA((len(edges),)))
    if staged:
        scratch += [pltpu.VMEM((rows_out, frames, width, channels), jnp.bfloat16), pltpu.SemaphoreType.DMA((1,))]
        held += 2 * frames * width * channels * rows_out
    return pl.pallas_call(
        functools.partial(stage_kernel, plan),
        out_shape=[
            jax.ShapeDtypeStruct(shape, jnp.float32 if number in in_float else jnp.bfloat16)
            for number, shape in enumerate(out_shapes)
        ],
        in_specs=[pl.BlockSpec(memory_space=space) for space in spaces],
        out_specs=[pl.BlockSpec(memory_space=space) for space in out_spaces],
        scratch_shapes=scratch,
        input_output_aliases={} if into is None else {len(args) - 1: 0},
        compiler_params=pltpu.CompilerParams(vmem_limit_bytes=held + 12 * MIB),
        cost_estimate=pl.CostEstimate(flops=flops, bytes_accessed=1024, transcendentals=0),
        name=name,
    )(*args)


def arrive_kernel(plan, *refs):
    pair_ref, own_ref, part_ref, time_ref, w_ref, _, out_ref = refs[:7]
    refs = list(refs[7:])
    later_ref = refs.pop(0) if plan["later"] else None
    x_ref, act_ref, stage_ref, sem = refs
    count, frames, width, channels = x_ref.shape
    depth = pair_ref.shape[3]
    before, latest = [pair_ref[:, frame].reshape(count * width, depth) for frame in range(2)]
    copies = []
    for pair in range(2):
        total = own_ref[plan["own_at"] : plan["own_at"] + count, pair].reshape(count * width, 2 * channels)
        if pair == 0:
            total += jnp.dot(before, time_ref[0], preferred_element_type=jnp.float32)
            total += jnp.dot(latest, time_ref[1], preferred_element_type=jnp.float32)
        else:
            total += jnp.dot(latest, time_ref[0], preferred_element_type=jnp.float32)
        total = total.astype(jnp.bfloat16)
        for half in range(2):
            x_ref[:, 2 * pair + half] = total[:, half * channels : (half + 1) * channels].reshape(
                count, width, channels
            )
            for row in range(count):
                activate(x_ref, act_ref, row, 2 * pair + half)
        if pair == 0 and count > 1:
            continue
        both = slice(2 * pair, 2 * pair + 2) if count == 1 else slice(0, frames)
        wide = both.stop - both.start
        place = 0
        for later, index, part, residual, taps in plan["terms"]:
            total = None
            for tap, row in taps:
                lhs = act_ref[row, both].reshape(wide * width, 3 * channels)
                value = jnp.dot(lhs, w_ref[tap], preferred_element_type=jnp.float32)
                total = value if total is None else total + value
            total = total.reshape(wide, width, channels)
            if part is not None:
                total += part_ref[part, both]
            if residual is not None:
                total += x_ref[residual, both].astype(jnp.float32)
            if later:
                later_ref[index, both] = total
                continue
            stage_ref[place, both] = total.astype(jnp.bfloat16)
            copies.append(
                pltpu.make_async_copy(stage_ref.at[place, both], out_ref.at[both, index], sem.at[len(copies)])
            )
            copies[-1].start()
            place += 1
    for copy in copies:
        copy.wait()


def arrive(name, pair, own, own_at, part, time, weight, into, terms):
    count = pair.shape[0]
    _, frames, width, channels = part.shape
    later = sum(term[0] for term in terms)
    final = len(terms) - later
    shapes = [jax.ShapeDtypeStruct(into.shape, into.dtype)]
    if later:
        shapes.append(jax.ShapeDtypeStruct((later,) + part.shape[1:], jnp.float32))
    return pl.pallas_call(
        functools.partial(arrive_kernel, dict(terms=terms, own_at=own_at, later=later)),
        out_shape=shapes,
        in_specs=[pl.BlockSpec(memory_space=pltpu.VMEM)] * 5 + [pl.BlockSpec(memory_space=pl.ANY)],
        out_specs=[pl.BlockSpec(memory_space=pltpu.HBM)] + [pl.BlockSpec(memory_space=pltpu.VMEM)] * (len(shapes) - 1),
        scratch_shapes=[
            pltpu.VMEM((count, frames, width, channels), jnp.bfloat16),
            pltpu.VMEM((count, frames, width, 3 * channels), jnp.bfloat16),
            pltpu.VMEM((final, frames, width, channels), jnp.bfloat16),
            pltpu.SemaphoreType.DMA((2 * final,)),
        ],
        input_output_aliases={5: 0},
        compiler_params=pltpu.CompilerParams(vmem_limit_bytes=16 * MIB),
        cost_estimate=pl.CostEstimate(
            flops=2 * frames * width * channels * (3 * len(terms) * channels + 2 * count * time.shape[1]),
            bytes_accessed=1024,
            transcendentals=0,
        ),
        name=name,
    )(pair, own, part, time, weight, into)


def to_next(value, axis):
    count = lax.axis_size(axis)
    return lax.ppermute(value, axis, [(i, i + 1) for i in range(count - 1)])


def to_previous(value, axis):
    count = lax.axis_size(axis)
    return lax.ppermute(value, axis, [(i + 1, i) for i in range(count - 1)])


def on_device(frames, space_weight, time_weight, out_weight):
    count, rows, width, channels = frames.shape
    depth = time_weight.shape[3]
    space = space_weight.reshape(3, 3 * channels, channels)
    time = time_weight.reshape(3, channels, 2 * depth)
    out_w = out_weight.reshape(3, 3 * depth, depth)
    wide = (count, width, channels)
    fine = (2 * count, width, depth)
    last = rows - 1

    def chunk(n):
        return (n, count, width, channels)

    def lifted(n):
        return (n, 2 * count, width, depth)

    here = pltpu.with_memory_space_constraint(frames, pltpu.HBM)
    space_here = pltpu.with_memory_space_constraint(space, pltpu.HBM)
    (ha,) = stage(
        "hidden_1_2", [here], space_here, [(0, 0, 4, 0)], [(0, 2, 0, 0, 0)], [chunk(2)], wide, fetched=True, fetch=True
    )
    pa = to_next(ha, "tm")
    (hb,) = stage(
        "hidden_3_6",
        [here],
        space,
        [(0, 2, 6, 0)],
        [(0, 4, 0, 0, 0)],
        [chunk(4)],
        wide,
        fetched=True,
        after=[ha],
    )
    pb = to_next(hb, "tm")
    hc, first_row, last_row = stage(
        "hidden_7_10",
        [here],
        space,
        [(0, 6, 6, 0)],
        [(0, 4, 0, 0, 0)],
        [chunk(4)],
        wide,
        fetched=True,
        after=[hb],
        edges=(0, last),
    )
    pc = to_next(hc, "tm")
    above = to_next(last_row, "rows")
    below = to_previous(first_row, "rows")
    hd, he, hf = stage(
        "hidden_rest",
        [here, above, below],
        space,
        [(1, 0, 1, 0), (0, 0, 2, 1), (0, 10, 6, 3), (2, 0, 1, 9)],
        [(0, 1, 0, 0, 1), (3, 2, 0, 1, 0), (5, 1, 2, 2, 0), (6, 1, 2, 1, 2), (7, 1, 2, 0, 0)],
        [chunk(2), chunk(3), chunk(1)],
        wide,
        fetched=True,
        after=[hc, pa],
    )
    pd = to_next(hd, "tm")
    pe = to_next(he, "tm")
    pf = to_next(hf, "tm")

    whole = (2 * count, rows, width, depth)
    out, ua, ub = stage(
        "out_2_5",
        [ha, pa, hb, pb],
        out_w,
        [],
        [(0, 4, 0, 0, 2)],
        [whole, lifted(2), lifted(2)],
        fine,
        staged=True,
        lifts=[(0, 1, 0, 2, 0), (2, 3, 0, 4, 2)],
        time=time,
        keeps=[(1, 0, 2), (2, 4, 2)],
        after=[hd],
    )
    out, uc = stage(
        "out_6_9",
        [hc, pc, ub],
        out_w,
        [(2, 0, 2, 0)],
        [(0, 4, 0, 0, 6)],
        [whole, lifted(2)],
        fine,
        staged=True,
        lifts=[(0, 1, 0, 4, 2)],
        time=time,
        keeps=[(1, 4, 2)],
        into=out,
    )
    ud = upsample("up_edges", hd, pd, time, depth, uc)
    up_above = to_next(ud[:1], "rows")
    up_below = to_previous(ud[1:], "rows")
    out, part, own = stage(
        "out_0_1",
        [ua, ud, up_above, uc, up_below, he, hf],
        out_w,
        [(2, 0, 1, 0), (1, 1, 1, 1), (0, 0, 2, 2), (3, 0, 2, 4), (1, 0, 1, 6), (4, 0, 1, 7)],
        [(0, 2, 0, 0, 0)],
        [whole, (4,) + lifted(1)[1:], (4, 2, width, 2 * depth)],
        fine,
        staged=True,
        into=out,
        time=time,
        prepared=(4, 5, 6, 7),
        partials=[
            (1, 0, 5, ((0, 4), (1, 5))),
            (1, 1, None, ((0, 5),)),
            (1, 2, None, ((2, 6),)),
            (1, 3, 6, ((1, 6), (2, 7))),
        ],
        own_parts=[(5, 0, 3, 2, 0), (6, 0, 1, 2, 3)],
    )
    out, last_part = arrive(
        "out_10_15",
        pe,
        own,
        0,
        part,
        time,
        out_w,
        out,
        [
            (False, 10, 0, None, ((2, 0),)),
            (False, 11, 1, 0, ((1, 0), (2, 1))),
            (False, 15, 3, None, ((0, 2),)),
            (True, 0, None, 1, ((0, 0), (1, 1))),
            (True, 1, None, None, ((0, 1), (2, 2))),
            (True, 2, 2, 2, ((1, 2),)),
        ],
    )
    (out,) = arrive(
        "out_12_14",
        pf,
        own,
        3,
        last_part,
        time,
        out_w,
        out,
        [
            (False, 12, 0, None, ((2, 0),)),
            (False, 13, 1, 0, ((1, 0),)),
            (False, 14, 2, None, ((0, 0),)),
        ],
    )
    return out


def upsample_kernel(own_ref, prev_ref, w_ref, _, out_ref):
    rows, _, width, channels = own_ref.shape
    depth = out_ref.shape[3]
    size = rows * width
    window = [
        prev_ref[:, 0].reshape(size, channels),
        prev_ref[:, 1].reshape(size, channels),
        own_ref[:, 0].reshape(size, channels),
        own_ref[:, 1].reshape(size, channels),
    ]
    for frame in range(2):
        total = jnp.dot(window[frame], w_ref[0], preferred_element_type=jnp.float32)
        for tap in (1, 2):
            total += jnp.dot(window[frame + tap], w_ref[tap], preferred_element_type=jnp.float32)
        total = total.astype(jnp.bfloat16)
        for half in range(2):
            out_ref[:, 2 * frame + half] = total[:, half * depth : (half + 1) * depth].reshape(
                rows, width, depth
            )


def upsample(name, own, prev, weight, depth, after):
    rows, frames, width, channels = own.shape
    return pl.pallas_call(
        upsample_kernel,
        out_shape=jax.ShapeDtypeStruct((rows, 2 * frames, width, depth), jnp.bfloat16),
        in_specs=[pl.BlockSpec(memory_space=pltpu.VMEM)] * 3 + [pl.BlockSpec(memory_space=pltpu.HBM)],
        out_specs=pl.BlockSpec(memory_space=pltpu.VMEM),
        compiler_params=pltpu.CompilerParams(vmem_limit_bytes=12 * MIB),
        cost_estimate=pl.CostEstimate(
            flops=2 * rows * frames * width * 3 * channels * 2 * depth,
            bytes_accessed=2 * rows * frames * width * (2 * channels + 2 * depth) + 2 * weight.size,
            transcendentals=0,
        ),
        name=name,
    )(own, prev, weight, after)


def solution(mesh):
    return jax.shard_map(
        on_device,
        mesh=mesh,
        in_specs=(P("tm", "rows", None, None), P(), P(), P()),
        out_specs=P("tm", "rows", None, None),
        check_vma=False,
    )
```
